128 devices in a mesh: tile: 8 (over y_hi, x), orient: 16 (over z, y_lo, core).
Axes of the slice: x: 4, y: 4 (y_hi: 2, y_lo: 2; y = y_hi * 2 + y_lo), z: 4, core: 2. Of those that a mesh axis runs over, the one named last changes fastest.
Arguments:
- tile_images: bfloat16 [32, 256, 256], P('tile', 'orient'), may hold values from -6 to 6
- templates: bfloat16 [192, 128, 128], P('orient'), may hold values from -6 to 6
- filters: float32 [8, 256, 256], P('tile'), may hold values from 0.25 to 4
- tile_bins: int32 [32], replicated, may hold values from 0 to 7, as said below
Outputs:
- best_snr: float32 [32, 256, 256], P('tile', 'orient')
The draws below stay inside these ranges and needn't reach their ends.
Inputs may be any that keep to these rules, and one draw needn't show every extreme that they name: `tile_bins`: every bin is named by 1 to 8 tiles, and one bin by exactly 8.
All inputs are finite; a program needn't handle non-finite values.
Results may differ from the reference program's by a relative error of at most 0.0031.
Values may be sent and summed in bfloat16 or wider, within the bound.
No kernel may reach another device: no remote copies, remote signals or barrier semaphores. Data moves between devices by JAX's collectives and lax.ppermute only.
A program may use at most 64 MiB of HBM per device.

```python
import math
import jax
import jax.numpy as jnp
from jax import lax

S = 256
P_SIZE = 128
ORIENT_DEV = 12
ORIENTS = 192
TILES = 32
BINS = 8
CAPG = 8
N_TILE = 8
N_ORIENT = 16


def draw_tile_bins(key, part):
    key = jax.random.fold_in(key, 7)
    first_key, second_key, third_key = jax.random.split(key, 3)
    slot_total = N_TILE * CAPG
    favoured = jax.random.randint(first_key, (), 0, N_TILE)
    slot_ids = jnp.arange(slot_total, dtype=jnp.int32)
    owner_bin = slot_ids // CAPG
    needed = (slot_ids % CAPG == 0) | (owner_bin == favoured)
    priority = jax.random.permutation(second_key, slot_total).astype(jnp.int32) + jnp.where(needed, 0, slot_total).astype(jnp.int32)
    sorted_slots = jnp.argsort(priority, stable=True)
    chosen = owner_bin[sorted_slots[:TILES]]
    shuffle = jax.random.permutation(third_key, TILES)
    return chosen[shuffle].astype(jnp.int32)


def steps_of(own_key, dims, cuts, smallest, largest):
    gain = 1.0
    for dim, shards_of in cuts:
        steps = jax.random.uniform(jax.random.fold_in(jax.random.fold_in(own_key, 6), dim), (shards_of,), jnp.float32, smallest / len(cuts), largest / len(cuts))
        gain = gain * jnp.repeat(jnp.exp(steps), dims[dim] // shards_of).reshape((-1,) + (1,) * (len(dims) - 1 - dim))
    return gain


def gaussian(rng, extent, width, most, cuts=(), kind=jnp.bfloat16):
    level = steps_of(rng, extent, cuts, -0.22, 0.18) if cuts else 1.0
    array = jax.random.normal(rng, extent, jnp.float32) * width * level
    return jnp.minimum(jnp.maximum(array, -most), most).astype(kind)


def setup_inputs(seed: int = 0) -> dict:
    arg_keys = jax.random.split(jax.random.key(seed), 5)
    return {
        "tile_images": gaussian(arg_keys[0], (TILES, S, S), 1.0, 6.0, ((0, 8), (1, 16))),
        "templates": gaussian(arg_keys[1], (ORIENTS, P_SIZE, P_SIZE), 1.0, 6.0, ((0, 16),)),
        "filters": jnp.clip(jnp.exp(math.log(4.0) - 2.7725887 * jax.random.uniform(arg_keys[2], (BINS, S, S), jnp.float32) ** steps_of(arg_keys[2], (BINS, S, S), ((0, 8),), -0.2, 0.2)), 0.25, 4.0),
        "tile_bins": draw_tile_bins(jax.random.fold_in(arg_keys[4], 71), 0),
    }


def tables(side_length, count):
    row_index = jnp.arange(side_length, dtype=jnp.int32)[:, None]
    col_index = jnp.arange(count, dtype=jnp.int32)[None, :]
    phases = (row_index * col_index % side_length).astype(jnp.float32) * (2.0 * math.pi / side_length)
    return (jnp.cos(phases).astype(jnp.bfloat16), jnp.sin(phases).astype(jnp.bfloat16))

def contract(pattern, first_op, second_op):
    return jnp.einsum(pattern, first_op.astype(jnp.float32), second_op.astype(jnp.float32))

def correlate(spec_re, spec_im, temp_re, temp_im, filter_map, cosine, sine):
    tile_re = spec_re.astype(jnp.float32)[None]
    tile_im = spec_im.astype(jnp.float32)[None]
    proj_re = temp_re.astype(jnp.float32)
    proj_im = temp_im.astype(jnp.float32)
    prod_re = ((proj_re * tile_re + proj_im * tile_im) * filter_map).astype(jnp.bfloat16)
    prod_im = ((proj_re * tile_im - proj_im * tile_re) * filter_map).astype(jnp.bfloat16)
    half_re = (contract('xk,oky->oxy', cosine, prod_re) - contract('xk,oky->oxy', sine, prod_im)).astype(jnp.bfloat16)
    half_im = (contract('xk,oky->oxy', cosine, prod_im) + contract('xk,oky->oxy', sine, prod_re)).astype(jnp.bfloat16)
    correlation = contract('oxk,ky->oxy', half_re, cosine) - contract('oxk,ky->oxy', half_im, sine)
    norm_scale = lax.rsqrt(lax.optimization_barrier(jnp.mean(correlation * correlation, axis=(1, 2), keepdims=True)) + 1e-06)
    return lax.optimization_barrier(jnp.max(correlation * norm_scale, axis=0))

def reference(tile_images, templates, filters, tile_bins):
    cosine, sine = tables(S, S)
    cos_part, sin_part = tables(S, P_SIZE)
    row_re = contract('tak,ky->tay', tile_images, cosine).astype(jnp.bfloat16)
    row_im = (-contract('tak,ky->tay', tile_images, sine)).astype(jnp.bfloat16)
    spec_re = (contract('xa,tay->txy', cosine, row_re) + contract('xa,tay->txy', sine, row_im)).astype(jnp.bfloat16)
    spec_im = (contract('xa,tay->txy', cosine, row_im) - contract('xa,tay->txy', sine, row_re)).astype(jnp.bfloat16)
    temp_row_re = contract('oak,yk->oay', templates, cos_part).astype(jnp.bfloat16)
    temp_row_im = (-contract('oak,yk->oay', templates, sin_part)).astype(jnp.bfloat16)
    temp_re = (contract('xa,oay->oxy', cos_part, temp_row_re) + contract('xa,oay->oxy', sin_part, temp_row_im)).astype(jnp.bfloat16)
    temp_im = (contract('xa,oay->oxy', cos_part, temp_row_im) - contract('xa,oay->oxy', sin_part, temp_row_re)).astype(jnp.bfloat16)
    blocks_re = temp_re.reshape(N_ORIENT, ORIENT_DEV, S, S)
    blocks_im = temp_im.reshape(N_ORIENT, ORIENT_DEV, S, S)
    tile_filters = jnp.take(filters, tile_bins.astype(jnp.int32), axis=0)

    def one_tile(record):
        tile_re, tile_im, filter_map = record

        def fold_step(running, batch_pair):
            return (jnp.maximum(running, correlate(tile_re, tile_im, batch_pair[0], batch_pair[1], filter_map, cosine, sine)), None)
        initial = jnp.full((S, S), -jnp.inf, dtype=jnp.float32)
        running, _ = lax.scan(fold_step, initial, (blocks_re, blocks_im))
        return running
    return lax.map(one_tile, (spec_re, spec_im, tile_filters))
```

```python
import functools

import jax
import jax.numpy as jnp
import ml_dtypes
import numpy as np
from jax import lax
from jax.experimental import pallas as pl
from jax.experimental.pallas import tpu as pltpu
from jax.sharding import Mesh
from jax.sharding import PartitionSpec as P

BF = jnp.bfloat16
F32 = jnp.float32
S = 256
Q = 128
HR = 144
OD = 12
MAXB = 24


def tables():
    idx = np.arange(S)
    phase = 2.0 * np.pi * ((idx[:, None] * idx[None, :]) % S) / S
    cos = np.cos(phase).astype(ml_dtypes.bfloat16).astype(np.float32)
    sin = np.sin(phase).astype(ml_dtypes.bfloat16).astype(np.float32)
    return cos, sin


def constants():
    c, s = tables()
    cat = np.concatenate
    bf = lambda a: np.asarray(a, np.float32).astype(ml_dtypes.bfloat16)
    row = bf(cat([c, -s], 1))
    col = bf(cat([c, s], 1)[:HR])
    trow = bf(cat([c[:Q], -s[:Q]], 1))
    tcol = bf(cat([c[:, :Q], s[:, :Q]], 1)[:HR])
    inv1 = bf(cat([cat([c, s], 1), cat([-s, c], 1)], 0))
    wre = 2.0 * c[:, :Q]
    wre[:, 0] = c[:, 0]
    wim = -2.0 * s[:, :Q]
    wim[:, 0] = c[:, Q]
    inv2 = bf(cat([wre, wim], 1))
    flip = np.zeros((S, S), np.float32)
    flip[np.arange(S), (-np.arange(S)) % S] = 1.0
    return row, col, trow, tcol, inv1, inv2, bf(flip)


def dot(a, b):
    return jnp.dot(a, b, preferred_element_type=F32)


def filter_kernel(core_ref, f_ref, flip_ref, out_ref):
    f = f_ref[...]
    hi = f.astype(BF)
    lo = (f - hi.astype(F32)).astype(BF)
    flip = flip_ref[...]
    rows = flip[:HR]
    turned = dot(dot(rows, hi).astype(BF), flip) + dot(dot(rows, lo).astype(BF), flip)
    sym = (0.5 * (f[:HR] + turned)).astype(BF)
    out_ref[...] = jnp.where(core_ref[0] == 0, sym[:, :Q], sym[:, Q:])


def template_kernel(t_ref, trow_ref, tcol_ref, out_ref, nyq_ref, rhs_ref):
    count = t_ref.shape[0]
    rows = dot(t_ref[...].reshape(count * Q, Q), trow_ref[...]).astype(BF)
    for o in range(count):
        re = rows[o * Q : (o + 1) * Q, :S]
        im = rows[o * Q : (o + 1) * Q, S:]
        rhs_ref[o, :Q, :S] = re
        rhs_ref[o, :Q, S:] = im
        rhs_ref[o, Q:, :S] = im
        rhs_ref[o, Q:, S:] = -re
        spec = dot(tcol_ref[...], rhs_ref[o])
        out_ref[o] = spec[:Q].astype(BF)
        first = lax.broadcasted_iota(jnp.int32, (8, 2 * S), 0) == 0
        nyq_ref[o] = jnp.where(first, spec[Q : Q + 8].astype(BF).astype(F32), 0.0)


def main_kernel(
    meta_ref, img_ref, fil_ref, t0_ref, t1_ref, n0_ref, n1_ref,
    row_ref, col_ref, inv1_ref, inv2_ref,
    out_ref,
    x_ref, r_ref, h_ref, hn_ref, p_ref, q_ref, c_ref,
):
    step = pl.program_id(0)

    @pl.when(step == 0)
    def _():
        z, yl, core = meta_ref[0], meta_ref[1], meta_ref[2]
        for t in range(2):
            for zs in range(4):
                for ys in range(2):
                    for cs in range(2):
                        block = (
                            ((z - zs + 4) % 4) * 4
                            + (yl + ys) % 2 * 2
                            + (core + cs) % 2
                        )
                        at = pl.multiple_of(block * 16, 16)
                        x_ref[t, pl.ds(at, 16), :] = img_ref[zs, ys, cs, t]
        for t in range(2):
            rows = dot(x_ref[t], row_ref[...]).astype(BF)
            re, im = rows[:, :S], rows[:, S:]
            r_ref[:S, :S] = re
            r_ref[:S, S:] = im
            r_ref[S:, :S] = im
            r_ref[S:, S:] = -re
            spec = dot(col_ref[...], r_ref[...])
            slot = meta_ref[3 + t]
            f_lo = fil_ref[core, slot].astype(F32)
            f_hi = fil_ref[1 - core, slot].astype(F32)
            f = jnp.concatenate([f_lo, f_hi, f_lo, f_hi], axis=1)
            spec = spec * f
            h_ref[t] = spec[:Q]
            hn_ref[t] = spec[Q : Q + 8]
        out_ref[...] = jnp.full(out_ref.shape, -jnp.inf, F32)

    temps = [(t0_ref, n0_ref, k) for k in range(t0_ref.shape[0])]
    temps += [(t1_ref, n1_ref, k) for k in range(t1_ref.shape[0])]
    for t in range(2):
        hr, hi = h_ref[t, :, :S], h_ref[t, :, S:]
        mr, mi = hn_ref[t, :, :S], hn_ref[t, :, S:]
        for j, (t_ref, n_ref, k) in enumerate(temps):
            tr = t_ref[k, :, :S].astype(F32)
            ti = t_ref[k, :, S:].astype(F32)
            nr, ni = n_ref[k, :, :S], n_ref[k, :, S:]
            pr = tr * hr + ti * hi
            pi = tr * hi - ti * hr
            pr0 = pr[:8] - (nr * mi - ni * mr)
            pi0 = pi[:8] + (nr * mr + ni * mi)
            pr = jnp.concatenate([pr0, pr[8:]], axis=0)
            pi = jnp.concatenate([pi0, pi[8:]], axis=0)
            p_ref[j * Q : (j + 1) * Q, :S] = pr.astype(BF)
            p_ref[j * Q : (j + 1) * Q, S:] = pi.astype(BF)
        half = dot(p_ref[...], inv1_ref[...]).astype(BF)
        for j in range(len(temps)):
            q_ref[j, :Q] = half[j * Q : (j + 1) * Q, :S]
            q_ref[j, Q:] = half[j * Q : (j + 1) * Q, S:]
        for j in range(len(temps)):
            corr = dot(inv2_ref[...], q_ref[j])
            c_ref[j] = corr
            power = jnp.sum(corr * corr) * (1.0 / (S * S))
            scale = lax.rsqrt(power + 1e-06)
            best = out_ref[:, t].reshape(S, S)
            out_ref[:, t] = jnp.maximum(best, c_ref[j] * scale).reshape(16, 16, S)


def shards(tile_images, templates, filters, tile_bins):
    row, col, trow, tcol, inv1, inv2, flip = [jnp.asarray(a) for a in constants()]
    yh, x = lax.axis_index("yh"), lax.axis_index("x")
    z, yl, core = lax.axis_index("z"), lax.axis_index("yl"), lax.axis_index("c")
    swap = [(0, 1), (1, 0)]
    ring = lambda s: [(i, (i + s) % 4) for i in range(4)]
    core1 = core.reshape(1)
    smem = pl.BlockSpec(memory_space=pltpu.SMEM)
    vmem = pl.BlockSpec(memory_space=pltpu.VMEM)

    fil = pl.pallas_call(
        filter_kernel,
        out_shape=jax.ShapeDtypeStruct((HR, Q), BF),
        in_specs=[smem, vmem, vmem],
        out_specs=vmem,
        name="filter",
    )(core1, filters[0], flip)
    other_templates = lax.ppermute(templates, "c", swap)
    keep = lax.dynamic_slice_in_dim(tile_images, 2 * core, 2, 0)
    give = lax.dynamic_slice_in_dim(tile_images, 2 - 2 * core, 2, 0)
    img = jnp.stack([keep, lax.ppermute(give, "c", swap)])
    pairs = [(0, 3), (3, 0), (1, 2), (2, 1)]
    fil = jnp.stack([fil, lax.ppermute(fil, ("yh", "yl"), pairs)])
    img = jnp.stack([img, lax.ppermute(img, "yl", swap)])
    fil = jnp.stack([fil] + [lax.ppermute(fil, "x", ring(s)) for s in (1, 2, 3)])
    img = jnp.stack([img] + [lax.ppermute(img, "z", ring(s)) for s in (1, 2, 3)])
    fil = jnp.stack([fil, lax.ppermute(fil, "c", swap)]).reshape(2, 8, HR, Q)

    def spectra(t):
        return pl.pallas_call(
            template_kernel,
            grid=(3,),
            out_shape=(
                jax.ShapeDtypeStruct((OD, Q, 2 * S), BF),
                jax.ShapeDtypeStruct((OD, 8, 2 * S), F32),
            ),
            in_specs=[pl.BlockSpec((4, Q, Q), lambda i: (i, 0, 0)), vmem, vmem],
            out_specs=(
                pl.BlockSpec((4, Q, 2 * S), lambda i: (i, 0, 0)),
                pl.BlockSpec((4, 8, 2 * S), lambda i: (i, 0, 0)),
            ),
            scratch_shapes=[pltpu.VMEM((4, 2 * Q, 2 * S), BF)],
            cost_estimate=pl.CostEstimate(
                flops=OD * 2 * 40_000_000, bytes_accessed=2_000_000, transcendentals=0
            ),
            name="templates",
        )(t, trow, tcol)

    t0, n0 = spectra(templates)
    t1, n1 = spectra(other_templates)

    own = lax.dynamic_slice_in_dim(tile_bins, (yh * 4 + x) * 4 + 2 * core, 2, 0)
    slots = ((x - own % 4 + 4) % 4) * 2 + (own // 4 + yh) % 2
    meta = jnp.concatenate([jnp.stack([z, yl, core]), slots])

    nb = 2
    part = pl.pallas_call(
        main_kernel,
        grid=(OD // nb,),
        out_shape=jax.ShapeDtypeStruct((16, 2, 16, S), F32),
        in_specs=[
            smem, vmem, vmem,
            pl.BlockSpec((nb, Q, 2 * S), lambda i: (i, 0, 0)),
            pl.BlockSpec((nb, Q, 2 * S), lambda i: (i, 0, 0)),
            pl.BlockSpec((nb, 8, 2 * S), lambda i: (i, 0, 0)),
            pl.BlockSpec((nb, 8, 2 * S), lambda i: (i, 0, 0)),
            vmem, vmem, vmem, vmem,
        ],
        out_specs=pl.BlockSpec((16, 2, 16, S), lambda i: (0, 0, 0, 0)),
        scratch_shapes=[
            pltpu.VMEM((2, S, S), BF),
            pltpu.VMEM((2 * S, 2 * S), BF),
            pltpu.VMEM((2, Q, 2 * S), F32),
            pltpu.VMEM((2, 8, 2 * S), F32),
            pltpu.VMEM((2 * nb * Q, 2 * S), BF),
            pltpu.VMEM((2 * nb, S, S), BF),
            pltpu.VMEM((2 * nb, S, S), F32),
        ],
        compiler_params=pltpu.CompilerParams(vmem_limit_bytes=40 * 1024 * 1024),
        name="correlate",
    )(meta, img, fil, t0, t1, n0, n1, row, col, inv1, inv2)

    got = lax.all_to_all(part, ("z", "yl", "c"), 0, 0)
    return jnp.max(got.reshape(8, 4, 16, S), axis=0)


def solution(mesh):
    fine = Mesh(mesh.devices.reshape(2, 4, 4, 2, 2), ("yh", "x", "z", "yl", "c"))
    tile, orient = ("yh", "x"), ("z", "yl", "c")
    placed = (P(tile, orient, None), P(orient, None, None), P(tile, None, None), P())
    return jax.shard_map(
        shards, mesh=fine, in_specs=placed, out_specs=P(tile, orient, None), check_vma=False
    )
```

```python
import jax
import jax.numpy as jnp
import ml_dtypes
import numpy as np
from jax import lax
from jax.experimental import pallas as pl
from jax.experimental.pallas import tpu as pltpu
from jax.sharding import Mesh
from jax.sharding import PartitionSpec as P

BF = jnp.bfloat16
F32 = jnp.float32
S = 256
Q = 128
HR = 144
OD = 12
NB = 3
RC = 32
MIB = 1024 * 1024


def tables():
    idx = np.arange(S)
    phase = 2.0 * np.pi * ((idx[:, None] * idx[None, :]) % S) / S
    cos = np.cos(phase).astype(ml_dtypes.bfloat16).astype(np.float32)
    sin = np.sin(phase).astype(ml_dtypes.bfloat16).astype(np.float32)
    return cos, sin


def constants():
    c, s = tables()
    cat = np.concatenate
    bf = lambda a: np.asarray(a, np.float32).astype(ml_dtypes.bfloat16)
    row = bf(cat([c, -s], 1))
    col = bf(cat([c, s], 1)[:HR])
    trow = bf(cat([c[:Q], -s[:Q]], 1))
    tcol = bf(cat([c[:, :Q], s[:, :Q]], 1)[:HR])
    inv1 = bf(cat([cat([c, s], 1), cat([-s, c], 1)], 0))
    wre = 2.0 * c[:, :Q]
    wre[:, 0] = c[:, 0]
    wim = -2.0 * s[:, :Q]
    wim[:, 0] = c[:, Q]
    inv2 = bf(cat([wre, wim], 1))
    return row, col, trow, tcol, inv1, inv2


def dot(a, b):
    return jnp.dot(a, b, preferred_element_type=F32)


def place(index):
    return index // 64, index // 16 % 4, index // 4 % 4, index // 2 % 2, index % 2


def fetch(pairs, sems):
    copies = [pltpu.make_async_copy(a, b, sems.at[i]) for i, (a, b) in enumerate(pairs)]
    for copy in copies:
        copy.start()
    return copies


def prep_kernel(
    index_ref, f_hbm, img_hbm, t_hbm, trow_hbm, tcol_hbm,
    fil_ref, split_ref, t_ref, trow_ref, tcol_ref,
    f_ref, img_ref, sems,
):
    core = index_ref[0] % 2
    copies = fetch(
        [
            (img_hbm, img_ref),
            (f_hbm, f_ref),
            (t_hbm, t_ref),
            (trow_hbm, trow_ref),
            (tcol_hbm, tcol_ref),
        ],
        sems,
    )
    a = lax.broadcasted_iota(jnp.int32, (S, S), 0)
    b = lax.broadcasted_iota(jnp.int32, (S, S), 1)
    flip = jnp.where((a + b) % S == 0, 1.0, 0.0).astype(BF)
    copies[0].wait()
    split_ref[0] = img_ref[pl.ds(2 * core, 2)]
    split_ref[1] = img_ref[pl.ds(2 - 2 * core, 2)]
    copies[1].wait()
    f = f_ref[0]
    hi = f.astype(BF)
    lo = (f - hi.astype(F32)).astype(BF)
    rows = flip[:HR]
    turned = dot(dot(rows, hi).astype(BF), flip) + dot(dot(rows, lo).astype(BF), flip)
    sym = (0.5 * (f[:HR] + turned)).astype(BF)
    fil_ref[...] = jnp.where(core == 0, sym[:, :Q], sym[:, Q:])
    for copy in copies[2:]:
        copy.wait()


def template_kernel(t_ref, trow_ref, tcol_ref, out_ref, nyq_ref, rhs_ref):
    count = t_ref.shape[0]
    rows = dot(t_ref[...].reshape(count * Q, Q), trow_ref[...]).astype(BF)
    for o in range(count):
        re = rows[o * Q : (o + 1) * Q, :S]
        im = rows[o * Q : (o + 1) * Q, S:]
        rhs_ref[o, :Q, :S] = re
        rhs_ref[o, :Q, S:] = im
        rhs_ref[o, Q:, :S] = im
        rhs_ref[o, Q:, S:] = -re
    first = lax.broadcasted_iota(jnp.int32, (8, 2 * S), 0) == 0
    for o in range(count):
        spec = dot(tcol_ref[...], rhs_ref[o])
        out_ref[o] = spec[:Q].astype(BF)
        nyq_ref[o] = jnp.where(first, spec[Q : Q + 8].astype(BF).astype(F32), 0.0)


def tile_kernel(index_ref, *refs):
    imgs, (row_ref, col_ref, spec_ref, x_ref, r_ref) = refs[:2], refs[2:]
    _, _, z, yl, core = place(index_ref[0])
    for t in range(2):
        for zs in range(4):
            for ys in range(2):
                for cs in range(2):
                    side = z if zs < 2 else 3 - z
                    if zs % 2:
                        side = side + 1 - side % 2 * 2
                    block = side * 4 + (yl + ys) % 2 * 2 + (core + cs) % 2
                    at = pl.multiple_of(block * 16, 16)
                    x_ref[t, pl.ds(at, 16), :] = imgs[cs][ys, zs // 2, zs % 2, t]
    for t in range(2):
        rows = dot(x_ref[t], row_ref[...]).astype(BF)
        re, im = rows[:, :S], rows[:, S:]
        r_ref[t, :S, :S] = re
        r_ref[t, :S, S:] = im
        r_ref[t, S:, :S] = im
        r_ref[t, S:, S:] = -re
    for t in range(2):
        spec_ref[t] = dot(col_ref[...], r_ref[t])


def main_kernel(
    index_ref, bins_ref, spec_ref, fa_ref, fb_ref,
    t0_ref, t1_ref, n0_ref, n1_ref, inv1_ref, inv2_ref,
    out_ref,
    h_ref, hn_ref, p_ref, q_ref, c_ref, s_ref,
):
    yh, x, _, _, core = place(index_ref[0])
    for t in range(2):
        name = bins_ref[(yh * 4 + x) * 4 + 2 * core + t]
        xs = (x // 2 + name % 4 // 2) % 2
        xn = (x + name + xs) % 2
        ys = (name // 4 + yh) % 2
        fa = fa_ref[xs, xn, ys].astype(F32)
        fb = fb_ref[xs, xn, ys].astype(F32)
        lo = jnp.where(core == 0, fa, fb)
        hi = jnp.where(core == 0, fb, fa)
        spec = spec_ref[t] * jnp.concatenate([lo, hi, lo, hi], axis=1)
        h_ref[t] = spec[:Q]
        hn_ref[t] = spec[Q : Q + 8]
    out_ref[...] = jnp.full(out_ref.shape, -jnp.inf, F32)

    count = 4 * NB

    def chunk(k, carry):
        for b in range(NB):
            o = k * NB + b
            for i, (t_ref, n_ref) in enumerate(((t0_ref, n0_ref), (t1_ref, n1_ref))):
                for r in range(0, Q, 16):
                    rows = slice(r, r + 16)
                    tr = t_ref[o, rows, :S].astype(F32)
                    ti = t_ref[o, rows, S:].astype(F32)
                    for t in range(2):
                        at = (b * 4 + i * 2 + t) * Q + r
                        hr, hi = h_ref[t, rows, :S], h_ref[t, rows, S:]
                        pr = tr * hr + ti * hi
                        pi = tr * hi - ti * hr
                        if r == 0:
                            nr, ni = n_ref[o, :, :S], n_ref[o, :, S:]
                            mr, mi = hn_ref[t, :, :S], hn_ref[t, :, S:]
                            pr0 = pr[:8] - (nr * mi - ni * mr)
                            pi0 = pi[:8] + (nr * mr + ni * mi)
                            pr = jnp.concatenate([pr0, pr[8:]], axis=0)
                            pi = jnp.concatenate([pi0, pi[8:]], axis=0)
                        p_ref[at : at + 16, :S] = pr.astype(BF)
                        p_ref[at : at + 16, S:] = pi.astype(BF)
        half = dot(p_ref[...], inv1_ref[...]).astype(BF)
        for j in range(count):
            q_ref[j, :Q] = half[j * Q : (j + 1) * Q, :S]
            q_ref[j, Q:] = half[j * Q : (j + 1) * Q, S:]
        for j in range(count):
            c_ref[j] = dot(inv2_ref[...], q_ref[j])
            power = jnp.zeros((8, Q), F32)
            for r in range(0, S, RC):
                part = c_ref[j, r : r + RC]
                part = part * part
                power += jnp.sum((part[:, :Q] + part[:, Q:]).reshape(RC // 8, 8, Q), axis=0)
            s_ref[j] = power
        total = jnp.sum(jnp.sum(s_ref[...], axis=1), axis=1, keepdims=True)
        scale = lax.rsqrt(total * (1.0 / (S * S)) + 1e-06)
        scales = [jnp.broadcast_to(scale[j : j + 1], (8, Q)) for j in range(count)]
        for t in range(2):
            for r in range(0, S, RC):
                spots = [(r + a, l * Q) for a in range(0, RC, 8) for l in range(2)]
                view = [
                    (row // 16, t, slice(row % 16, row % 16 + 8), slice(lane, lane + Q))
                    for row, lane in spots
                ]
                best = [out_ref[v] for v in view]
                for j in range(t, count, 2):
                    for i, (row, lane) in enumerate(spots):
                        corr = c_ref[j, row : row + 8, lane : lane + Q]
                        best[i] = jnp.maximum(best[i], corr * scales[j])
                for v, value in zip(view, best):
                    out_ref[v] = value
        return carry

    lax.fori_loop(0, OD // NB, chunk, 0)


def shards(tile_images, templates, filters, tile_bins):
    row, col, trow, tcol, inv1, inv2 = [jnp.asarray(a) for a in constants()]
    index = lax.axis_index(("yh", "x", "z", "yl", "c")).reshape(1)
    swap = [(0, 1), (1, 0)]
    ring = lambda s: [(i, (i + s) % 4) for i in range(4)]
    smem = pl.BlockSpec(memory_space=pltpu.SMEM)
    vmem = pl.BlockSpec(memory_space=pltpu.VMEM)
    hbm = pl.BlockSpec(memory_space=pltpu.HBM)
    tie = lax.optimization_barrier

    def spectra(t):
        return pl.pallas_call(
            template_kernel,
            out_shape=(
                jax.ShapeDtypeStruct((OD, Q, 2 * S), BF),
                jax.ShapeDtypeStruct((OD, 8, 2 * S), F32),
            ),
            in_specs=[vmem, vmem, vmem],
            out_specs=(vmem, vmem),
            scratch_shapes=[pltpu.VMEM((OD, 2 * Q, 2 * S), BF)],
            compiler_params=pltpu.CompilerParams(vmem_limit_bytes=16 * MIB),
            cost_estimate=pl.CostEstimate(
                flops=OD * 90_000_000, bytes_accessed=2_000_000, transcendentals=0
            ),
            name="templates",
        )(t, trow, tcol)

    like = lambda a: jax.ShapeDtypeStruct(a.shape, a.dtype)
    far = lambda a: pltpu.with_memory_space_constraint(a, pltpu.HBM)
    fil, img, own_templates, trow, tcol = pl.pallas_call(
        prep_kernel,
        out_shape=(
            jax.ShapeDtypeStruct((HR, Q), BF),
            jax.ShapeDtypeStruct((2, 2, 16, S), BF),
            like(templates),
            like(trow),
            like(tcol),
        ),
        in_specs=[smem] + [hbm] * 5,
        out_specs=(vmem,) * 5,
        scratch_shapes=[
            pltpu.VMEM((1, S, S), F32),
            pltpu.VMEM((4, 16, S), BF),
            pltpu.SemaphoreType.DMA((5,)),
        ],
        compiler_params=pltpu.CompilerParams(vmem_limit_bytes=8 * MIB),
        name="prep",
    )(index, far(filters), far(tile_images), far(templates), far(trow), far(tcol))
    near, across = [(0, 1), (1, 0), (2, 3), (3, 2)], [(0, 3), (3, 0), (1, 2), (2, 1)]
    fil_y = lax.ppermute(fil, ("yh", "yl"), across)
    img_z = lax.ppermute(img, "z", near)
    other_templates = lax.ppermute(own_templates, "c", swap)
    t0, n0 = spectra(own_templates)
    other_templates, img_z, fil_y, t0, n0 = tie((other_templates, img_z, fil_y, t0, n0))
    fil = jnp.stack([fil, fil_y])
    img = jnp.stack([img, img_z], axis=1)
    fil_x = lax.ppermute(fil, "x", near)
    img_z = lax.ppermute(img, "z", across)
    t1, n1 = spectra(other_templates)
    fil_x, img_z, t1, n1 = tie((fil_x, img_z, t1, n1))
    fil = jnp.stack([fil, fil_x])
    img = jnp.stack([img, img_z], axis=1)
    fil_x = lax.ppermute(fil, "x", across)
    img_y = lax.ppermute(img, "yl", swap)
    fil_x, img_y = tie((fil_x, img_y))
    fil_a = jnp.stack([fil, fil_x])
    img_a = jnp.stack([img, img_y], axis=1)
    img_b = lax.ppermute(img_a[1], "c", swap)
    fil_b = lax.ppermute(fil_a, "c", swap)
    spec = pl.pallas_call(
        tile_kernel,
        out_shape=jax.ShapeDtypeStruct((2, HR, 2 * S), F32),
        in_specs=[smem] + [vmem] * 4,
        out_specs=vmem,
        scratch_shapes=[pltpu.VMEM((2, S, S), BF), pltpu.VMEM((2, 2 * S, 2 * S), BF)],
        compiler_params=pltpu.CompilerParams(vmem_limit_bytes=8 * MIB),
        cost_estimate=pl.CostEstimate(
            flops=800_000_000, bytes_accessed=1_000_000, transcendentals=0
        ),
        name="tiles",
    )(index, img_a[0], img_b, row, col)
    fil_b, spec = tie((fil_b, spec))

    count = 4 * NB
    part = pl.pallas_call(
        main_kernel,
        out_shape=jax.ShapeDtypeStruct((16, 2, 16, S), F32),
        in_specs=[smem, smem] + [vmem] * 9,
        out_specs=vmem,
        scratch_shapes=[
            pltpu.VMEM((2, Q, 2 * S), F32),
            pltpu.VMEM((2, 8, 2 * S), F32),
            pltpu.VMEM((count * Q, 2 * S), BF),
            pltpu.VMEM((count, S, S), BF),
            pltpu.VMEM((count, S, S), F32),
            pltpu.VMEM((count, 8, Q), F32),
        ],
        compiler_params=pltpu.CompilerParams(vmem_limit_bytes=24 * MIB),
        name="correlate",
    )(index, tile_bins, spec, fil_a, fil_b, t0, t1, n0, n1, inv1, inv2)

    got = lax.all_to_all(part.astype(jnp.float16), ("z", "yl", "c"), 0, 0)
    return jnp.max(got.astype(F32).reshape(8, 4, 16, S), axis=0)


def solution(mesh):
    fine = Mesh(mesh.devices.reshape(2, 4, 4, 2, 2), ("yh", "x", "z", "yl", "c"))
    tile, orient = ("yh", "x"), ("z", "yl", "c")
    placed = (P(tile, orient, None), P(orient, None, None), P(tile, None, None), P())
    return jax.shard_map(
        shards, mesh=fine, in_specs=placed, out_specs=P(tile, orient, None), check_vma=False
    )
```

```python
import jax
import jax.numpy as jnp
import ml_dtypes
import numpy as np
from jax import lax
from jax.experimental import pallas as pl
from jax.experimental.pallas import tpu as pltpu
from jax.sharding import Mesh
from jax.sharding import PartitionSpec as P

BF = jnp.bfloat16
F32 = jnp.float32
S = 256
Q = 128
HR = 144
OD = 12
NB = 3
RC = 32
MIB = 1024 * 1024


def tables():
    idx = np.arange(S)
    phase = 2.0 * np.pi * ((idx[:, None] * idx[None, :]) % S) / S
    cos = np.cos(phase).astype(ml_dtypes.bfloat16).astype(np.float32)
    sin = np.sin(phase).astype(ml_dtypes.bfloat16).astype(np.float32)
    return cos, sin


def constants():
    c, s = tables()
    cat = np.concatenate
    bf = lambda a: np.asarray(a, np.float32).astype(ml_dtypes.bfloat16)
    even, odd = np.arange(0, S, 2), np.arange(1, S, 2)
    order = cat([even, odd])
    row = bf(cat([c[:, order], -s[:, order]], 1))
    col = bf(cat([c, s], 1)[:HR])
    trow = bf(cat([c[:Q, order], -s[:Q, order]], 1))
    tcol = bf(cat([c[:, :Q], s[:, :Q]], 1)[:HR])
    turn = lambda k: cat([cat([c[k, :Q], s[k, :Q]], 1), cat([-s[k, :Q], c[k, :Q]], 1)], 0)
    inv1 = bf(np.stack([turn(even), turn(odd)]))
    wre = 2.0 * c[:, :Q]
    wre[:, 0] = c[:, 0]
    wim = -2.0 * s[:, :Q]
    wim[:, 0] = c[:, Q]
    inv2 = bf(cat([wre, wim], 1))
    return row, col, trow, tcol, inv1, inv2


def dot(a, b):
    return jnp.dot(a, b, preferred_element_type=F32)


def place(index):
    return index // 64, index // 16 % 4, index // 4 % 4, index // 2 % 2, index % 2


def fetch(pairs, sems):
    copies = [pltpu.make_async_copy(a, b, sems.at[i]) for i, (a, b) in enumerate(pairs)]
    for copy in copies:
        copy.start()
    return copies


def prep_kernel(
    index_ref, f_hbm, img_hbm, t_hbm, trow_hbm, tcol_hbm,
    fil_ref, split_ref, t_ref, trow_ref, tcol_ref,
    f_ref, img_ref, sems,
):
    core = index_ref[0] % 2
    copies = fetch(
        [
            (img_hbm, img_ref),
            (f_hbm, f_ref),
            (t_hbm, t_ref),
            (trow_hbm, trow_ref),
            (tcol_hbm, tcol_ref),
        ],
        sems,
    )
    a = lax.broadcasted_iota(jnp.int32, (S, S), 0)
    b = lax.broadcasted_iota(jnp.int32, (S, S), 1)
    flip = jnp.where((a + b) % S == 0, 1.0, 0.0).astype(BF)
    copies[0].wait()
    split_ref[0] = img_ref[pl.ds(2 * core, 2)]
    split_ref[1] = img_ref[pl.ds(2 - 2 * core, 2)]
    copies[1].wait()
    f = f_ref[0]
    hi = f.astype(BF)
    lo = (f - hi.astype(F32)).astype(BF)
    rows = flip[:HR]
    turned = dot(dot(rows, hi).astype(BF), flip) + dot(dot(rows, lo).astype(BF), flip)
    sym = (0.5 * (f[:HR] + turned)).astype(BF)
    order = jnp.where(a == jnp.where(b < Q, 2 * b, 2 * b - (S - 1)), 1.0, 0.0).astype(BF)
    sym = dot(sym, order).astype(BF)
    fil_ref[...] = jnp.where(core == 0, sym[:, :Q], sym[:, Q:])
    for copy in copies[2:]:
        copy.wait()


def template_kernel(t_ref, trow_ref, tcol_ref, out_ref, nyq_ref, rhs_ref):
    count = t_ref.shape[0]
    rows = dot(t_ref[...].reshape(count * Q, Q), trow_ref[...]).astype(BF)
    for o in range(count):
        re = rows[o * Q : (o + 1) * Q, :S]
        im = rows[o * Q : (o + 1) * Q, S:]
        rhs_ref[o, :Q, :S] = re
        rhs_ref[o, :Q, S:] = im
        rhs_ref[o, Q:, :S] = im
        rhs_ref[o, Q:, S:] = -re
    first = lax.broadcasted_iota(jnp.int32, (8, 2 * S), 0) == 0
    for o in range(count):
        spec = dot(tcol_ref[...], rhs_ref[o])
        out_ref[o] = spec[:Q].astype(BF)
        nyq_ref[o] = jnp.where(first, spec[Q : Q + 8].astype(BF).astype(F32), 0.0)


def tile_kernel(index_ref, *refs):
    imgs, (row_ref, col_ref, spec_ref, x_ref, r_ref) = refs[:2], refs[2:]
    _, _, z, yl, core = place(index_ref[0])
    for t in range(2):
        for zs in range(4):
            for ys in range(2):
                for cs in range(2):
                    side = z if zs < 2 else 3 - z
                    if zs % 2:
                        side = side + 1 - side % 2 * 2
                    block = side * 4 + (yl + ys) % 2 * 2 + (core + cs) % 2
                    at = pl.multiple_of(block * 16, 16)
                    x_ref[t, pl.ds(at, 16), :] = imgs[cs][ys, zs // 2, zs % 2, t]
    for t in range(2):
        rows = dot(x_ref[t], row_ref[...]).astype(BF)
        re, im = rows[:, :S], rows[:, S:]
        r_ref[t, :S, :S] = re
        r_ref[t, :S, S:] = im
        r_ref[t, S:, :S] = im
        r_ref[t, S:, S:] = -re
    for t in range(2):
        spec_ref[t] = dot(col_ref[...], r_ref[t])


def main_kernel(
    index_ref, bins_ref, spec_ref, fa_ref, fb_ref,
    t0_ref, t1_ref, n0_ref, n1_ref, inv1_ref, inv2_ref,
    out_ref,
    h_ref, hn_ref, p_ref, e_ref, o_ref, q_ref, c_ref, s_ref,
):
    yh, x, _, _, core = place(index_ref[0])
    for t in range(2):
        name = bins_ref[(yh * 4 + x) * 4 + 2 * core + t]
        xs = (x // 2 + name % 4 // 2) % 2
        xn = (x + name + xs) % 2
        ys = (name // 4 + yh) % 2
        fa = fa_ref[xs, xn, ys].astype(F32)
        fb = fb_ref[xs, xn, ys].astype(F32)
        lo = jnp.where(core == 0, fa, fb)
        hi = jnp.where(core == 0, fb, fa)
        spec = spec_ref[t] * jnp.concatenate([lo, hi, lo, hi], axis=1)
        h_ref[t] = spec[:Q]
        hn_ref[t] = spec[Q : Q + 8]
    out_ref[...] = jnp.full(out_ref.shape, -jnp.inf, F32)

    count = 4 * NB

    def chunk(k, carry):
        for b in range(NB):
            o = k * NB + b
            for i, (t_ref, n_ref) in enumerate(((t0_ref, n0_ref), (t1_ref, n1_ref))):
                for r in range(0, Q, 16):
                    rows = slice(r, r + 16)
                    tr = t_ref[o, rows, :S].astype(F32)
                    ti = t_ref[o, rows, S:].astype(F32)
                    for t in range(2):
                        at = (b * 4 + i * 2 + t) * Q + r
                        hr, hi = h_ref[t, rows, :S], h_ref[t, rows, S:]
                        pr = tr * hr + ti * hi
                        pi = tr * hi - ti * hr
                        if r == 0:
                            nr, ni = n_ref[o, :, :S], n_ref[o, :, S:]
                            mr, mi = hn_ref[t, :, :S], hn_ref[t, :, S:]
                            pr0 = pr[:8] - (nr * mi - ni * mr)
                            pi0 = pi[:8] + (nr * mr + ni * mi)
                            pr = jnp.concatenate([pr0, pr[8:]], axis=0)
                            pi = jnp.concatenate([pi0, pi[8:]], axis=0)
                        pr, pi = pr.astype(BF), pi.astype(BF)
                        p_ref[0, at : at + 16, :Q] = pr[:, :Q]
                        p_ref[0, at : at + 16, Q:] = pi[:, :Q]
                        p_ref[1, at : at + 16, :Q] = pr[:, Q:]
                        p_ref[1, at : at + 16, Q:] = pi[:, Q:]
        e_ref[...] = dot(p_ref[0], inv1_ref[0])
        o_ref[...] = dot(p_ref[1], inv1_ref[1])
        for j in range(count):
            for r in range(0, Q, 16):
                at = j * Q + r
                for lane in (0, Q):
                    even = e_ref[at : at + 16, lane : lane + Q]
                    odd = o_ref[at : at + 16, lane : lane + Q]
                    q_ref[j, lane + r : lane + r + 16, :Q] = (even + odd).astype(BF)
                    q_ref[j, lane + r : lane + r + 16, Q:] = (even - odd).astype(BF)
        for j in range(count):
            c_ref[j] = dot(inv2_ref[...], q_ref[j])
            power = jnp.zeros((8, Q), F32)
            for r in range(0, S, RC):
                part = c_ref[j, r : r + RC]
                part = part * part
                power += jnp.sum((part[:, :Q] + part[:, Q:]).reshape(RC // 8, 8, Q), axis=0)
            s_ref[j] = power
        total = jnp.sum(jnp.sum(s_ref[...], axis=1), axis=1, keepdims=True)
        scale = lax.rsqrt(total * (1.0 / (S * S)) + 1e-06)
        scales = [jnp.broadcast_to(scale[j : j + 1], (8, Q)) for j in range(count)]
        for t in range(2):
            for r in range(0, S, RC):
                spots = [(r + a, l * Q) for a in range(0, RC, 8) for l in range(2)]
                view = [
                    (row // 16, t, slice(row % 16, row % 16 + 8), slice(lane, lane + Q))
                    for row, lane in spots
                ]
                best = [out_ref[v] for v in view]
                for j in range(t, count, 2):
                    for i, (row, lane) in enumerate(spots):
                        corr = c_ref[j, row : row + 8, lane : lane + Q]
                        best[i] = jnp.maximum(best[i], corr * scales[j])
                for v, value in zip(view, best):
                    out_ref[v] = value
        return carry

    lax.fori_loop(0, OD // NB, chunk, 0)


def shards(tile_images, templates, filters, tile_bins):
    row, col, trow, tcol, inv1, inv2 = [jnp.asarray(a) for a in constants()]
    index = lax.axis_index(("yh", "x", "z", "yl", "c")).reshape(1)
    swap = [(0, 1), (1, 0)]
    ring = lambda s: [(i, (i + s) % 4) for i in range(4)]
    smem = pl.BlockSpec(memory_space=pltpu.SMEM)
    vmem = pl.BlockSpec(memory_space=pltpu.VMEM)
    hbm = pl.BlockSpec(memory_space=pltpu.HBM)
    tie = lax.optimization_barrier

    def spectra(t):
        return pl.pallas_call(
            template_kernel,
            out_shape=(
                jax.ShapeDtypeStruct((OD, Q, 2 * S), BF),
                jax.ShapeDtypeStruct((OD, 8, 2 * S), F32),
            ),
            in_specs=[vmem, vmem, vmem],
            out_specs=(vmem, vmem),
            scratch_shapes=[pltpu.VMEM((OD, 2 * Q, 2 * S), BF)],
            compiler_params=pltpu.CompilerParams(vmem_limit_bytes=16 * MIB),
            cost_estimate=pl.CostEstimate(
                flops=OD * 90_000_000, bytes_accessed=2_000_000, transcendentals=0
            ),
            name="templates",
        )(t, trow, tcol)

    like = lambda a: jax.ShapeDtypeStruct(a.shape, a.dtype)
    far = lambda a: pltpu.with_memory_space_constraint(a, pltpu.HBM)
    fil, img, own_templates, trow, tcol = pl.pallas_call(
        prep_kernel,
        out_shape=(
            jax.ShapeDtypeStruct((HR, Q), BF),
            jax.ShapeDtypeStruct((2, 2, 16, S), BF),
            like(templates),
            like(trow),
            like(tcol),
        ),
        in_specs=[smem] + [hbm] * 5,
        out_specs=(vmem,) * 5,
        scratch_shapes=[
            pltpu.VMEM((1, S, S), F32),
            pltpu.VMEM((4, 16, S), BF),
            pltpu.SemaphoreType.DMA((5,)),
        ],
        compiler_params=pltpu.CompilerParams(vmem_limit_bytes=8 * MIB),
        name="prep",
    )(index, far(filters), far(tile_images), far(templates), far(trow), far(tcol))
    near, across = [(0, 1), (1, 0), (2, 3), (3, 2)], [(0, 3), (3, 0), (1, 2), (2, 1)]
    fil_y = lax.ppermute(fil, ("yh", "yl"), across)
    img_z = lax.ppermute(img, "z", near)
    other_templates = lax.ppermute(own_templates, "c", swap)
    t0, n0 = spectra(own_templates)
    other_templates, img_z, fil_y, t0, n0 = tie((other_templates, img_z, fil_y, t0, n0))
    fil = jnp.stack([fil, fil_y])
    img = jnp.stack([img, img_z], axis=1)
    fil_x = lax.ppermute(fil, "x", near)
    img_z = lax.ppermute(img, "z", across)
    t1, n1 = spectra(other_templates)
    fil_x, img_z, t1, n1 = tie((fil_x, img_z, t1, n1))
    fil = jnp.stack([fil, fil_x])
    img = jnp.stack([img, img_z], axis=1)
    fil_x = lax.ppermute(fil, "x", across)
    img_y = lax.ppermute(img, "yl", swap)
    fil_x, img_y = tie((fil_x, img_y))
    fil_a = jnp.stack([fil, fil_x])
    img_a = jnp.stack([img, img_y], axis=1)
    img_b = lax.ppermute(img_a[1], "c", swap)
    fil_b = lax.ppermute(fil_a, "c", swap)
    spec = pl.pallas_call(
        tile_kernel,
        out_shape=jax.ShapeDtypeStruct((2, HR, 2 * S), F32),
        in_specs=[smem] + [vmem] * 4,
        out_specs=vmem,
        scratch_shapes=[pltpu.VMEM((2, S, S), BF), pltpu.VMEM((2, 2 * S, 2 * S), BF)],
        compiler_params=pltpu.CompilerParams(vmem_limit_bytes=8 * MIB),
        cost_estimate=pl.CostEstimate(
            flops=800_000_000, bytes_accessed=1_000_000, transcendentals=0
        ),
        name="tiles",
    )(index, img_a[0], img_b, row, col)
    fil_b, spec = tie((fil_b, spec))

    count = 4 * NB
    part = pl.pallas_call(
        main_kernel,
        out_shape=jax.ShapeDtypeStruct((16, 2, 16, S), F32),
        in_specs=[smem, smem] + [vmem] * 9,
        out_specs=vmem,
        scratch_shapes=[
            pltpu.VMEM((2, Q, 2 * S), F32),
            pltpu.VMEM((2, 8, 2 * S), F32),
            pltpu.VMEM((2, count * Q, S), BF),
            pltpu.VMEM((count * Q, S), F32),
            pltpu.VMEM((count * Q, S), F32),
            pltpu.VMEM((count, S, S), BF),
            pltpu.VMEM((count, S, S), F32),
            pltpu.VMEM((count, 8, Q), F32),
        ],
        compiler_params=pltpu.CompilerParams(vmem_limit_bytes=24 * MIB),
        name="correlate",
    )(index, tile_bins, spec, fil_a, fil_b, t0, t1, n0, n1, inv1, inv2)

    got = lax.all_to_all(part.astype(jnp.float16), ("z", "yl", "c"), 0, 0)
    return jnp.max(got.astype(F32).reshape(8, 4, 16, S), axis=0)


def solution(mesh):
    fine = Mesh(mesh.devices.reshape(2, 4, 4, 2, 2), ("yh", "x", "z", "yl", "c"))
    tile, orient = ("yh", "x"), ("z", "yl", "c")
    placed = (P(tile, orient, None), P(orient, None, None), P(tile, None, None), P())
    return jax.shard_map(
        shards, mesh=fine, in_specs=placed, out_specs=P(tile, orient, None), check_vma=False
    )
```

```python
import jax
import jax.numpy as jnp
import ml_dtypes
import numpy as np
from jax import lax
from jax.experimental import pallas as pl
from jax.experimental.pallas import tpu as pltpu
from jax.sharding import Mesh
from jax.sharding import PartitionSpec as P

BF = jnp.bfloat16
F32 = jnp.float32
S = 256
Q = 128
HR = 144
OD = 12
NB = 3
RC = 32
MIB = 1024 * 1024


def tables():
    idx = np.arange(S)
    phase = 2.0 * np.pi * ((idx[:, None] * idx[None, :]) % S) / S
    cos = np.cos(phase).astype(ml_dtypes.bfloat16).astype(np.float32)
    sin = np.sin(phase).astype(ml_dtypes.bfloat16).astype(np.float32)
    return cos, sin


def constants():
    c, s = tables()
    cat = np.concatenate
    bf = lambda a: np.asarray(a, np.float32).astype(ml_dtypes.bfloat16)
    even, odd = np.arange(0, S, 2), np.arange(1, S, 2)
    order = cat([even, odd])
    row = bf(cat([c[:, order], -s[:, order]], 1))
    col = bf(cat([c, s], 1)[:HR])
    trow = bf(cat([c[:Q, order], -s[:Q, order]], 1))
    tcol = bf(cat([c[:, :Q], s[:, :Q]], 1)[:HR])
    turn = lambda k: cat([cat([c[k, :Q], s[k, :Q]], 1), cat([-s[k, :Q], c[k, :Q]], 1)], 0)
    inv1 = bf(np.stack([turn(even), turn(odd)]))
    wre = 2.0 * c[:, :Q]
    wre[:, 0] = c[:, 0]
    wim = -2.0 * s[:, :Q]
    wim[:, 0] = c[:, Q]
    inv2 = bf(cat([wre, wim], 1))
    return row, col, trow, tcol, inv1, inv2


def dot(a, b):
    return jnp.dot(a, b, preferred_element_type=F32)


def place(index):
    return index // 64, index // 16 % 4, index // 4 % 4, index // 2 % 2, index % 2


def fetch(pairs, sems):
    copies = [pltpu.make_async_copy(a, b, sems.at[i]) for i, (a, b) in enumerate(pairs)]
    for copy in copies:
        copy.start()
    return copies


def prep_kernel(
    index_ref, f_hbm, img_hbm, t_hbm, trow_hbm, tcol_hbm,
    fil_ref, split_ref, t_ref, trow_ref, tcol_ref,
    f_ref, img_ref, sems,
):
    core = index_ref[0] % 2
    copies = fetch(
        [
            (img_hbm, img_ref),
            (f_hbm, f_ref),
            (t_hbm, t_ref),
            (trow_hbm, trow_ref),
            (tcol_hbm, tcol_ref),
        ],
        sems,
    )
    a = lax.broadcasted_iota(jnp.int32, (S, S), 0)
    b = lax.broadcasted_iota(jnp.int32, (S, S), 1)
    ordered = jnp.where(b < Q, 2 * b, 2 * b - (S - 1))
    pick = lambda mask: jnp.where(mask, 1.0, 0.0).astype(BF)
    flip = pick((a + b) % S == 0)[:HR]
    same, turned = pick(a == ordered), pick((a + ordered) % S == 0)
    copies[0].wait()
    split_ref[0] = img_ref[pl.ds(2 * core, 2)]
    split_ref[1] = img_ref[pl.ds(2 - 2 * core, 2)]
    copies[1].wait()
    f = f_ref[0]
    hi = f.astype(BF)
    lo = (f - hi.astype(F32)).astype(BF)
    both = dot(flip, jnp.concatenate([hi, lo], axis=1)).astype(BF)
    terms = jnp.concatenate([hi[:HR], lo[:HR], both], axis=1)
    sums = dot(terms, jnp.concatenate([same, same, turned, turned], axis=0))
    sym = (0.5 * sums).astype(BF)
    fil_ref[...] = jnp.where(core == 0, sym[:, :Q], sym[:, Q:])
    for copy in copies[2:]:
        copy.wait()


def template_kernel(t_ref, trow_ref, tcol_ref, out_ref, nyq_ref, rhs_ref):
    count = t_ref.shape[0]
    rows = dot(t_ref[...].reshape(count * Q, Q), trow_ref[...]).astype(BF)
    for o in range(count):
        re = rows[o * Q : (o + 1) * Q, :S]
        im = rows[o * Q : (o + 1) * Q, S:]
        rhs_ref[o, :Q, :S] = re
        rhs_ref[o, :Q, S:] = im
        rhs_ref[o, Q:, :S] = im
        rhs_ref[o, Q:, S:] = -re
    first = lax.broadcasted_iota(jnp.int32, (8, 2 * S), 0) == 0
    for o in range(count):
        spec = dot(tcol_ref[...], rhs_ref[o])
        out_ref[o] = spec[:Q].astype(BF)
        nyq_ref[o] = jnp.where(first, spec[Q : Q + 8].astype(BF).astype(F32), 0.0)


def tile_kernel(index_ref, *refs):
    imgs, (row_ref, col_ref, spec_ref, x_ref, r_ref) = refs[:2], refs[2:]
    _, _, z, yl, core = place(index_ref[0])
    for t in range(2):
        for zs in range(4):
            for ys in range(2):
                for cs in range(2):
                    side = z if zs < 2 else 3 - z
                    if zs % 2:
                        side = side + 1 - side % 2 * 2
                    block = side * 4 + (yl + ys) % 2 * 2 + (core + cs) % 2
                    at = pl.multiple_of(block * 16, 16)
                    x_ref[t, pl.ds(at, 16), :] = imgs[cs][ys, zs // 2, zs % 2, t]
    for t in range(2):
        rows = dot(x_ref[t], row_ref[...]).astype(BF)
        re, im = rows[:, :S], rows[:, S:]
        r_ref[t, :S, :S] = re
        r_ref[t, :S, S:] = im
        r_ref[t, S:, :S] = im
        r_ref[t, S:, S:] = -re
    for t in range(2):
        spec_ref[t] = dot(col_ref[...], r_ref[t])


def main_kernel(
    index_ref, bins_ref, spec_ref, fa_ref, fb_ref,
    t0_ref, t1_ref, n0_ref, n1_ref, inv1_ref, inv2_ref,
    out_ref,
    h_ref, hn_ref, p_ref, e_ref, o_ref, q_ref, c_ref, s_ref,
):
    yh, x, _, _, core = place(index_ref[0])
    for t in range(2):
        name = bins_ref[(yh * 4 + x) * 4 + 2 * core + t]
        xs = (x // 2 + name % 4 // 2) % 2
        xn = (x + name + xs) % 2
        ys = (name // 4 + yh) % 2
        fa = fa_ref[xs, xn, ys].astype(F32)
        fb = fb_ref[xs, xn, ys].astype(F32)
        lo = jnp.where(core == 0, fa, fb)
        hi = jnp.where(core == 0, fb, fa)
        spec = spec_ref[t] * jnp.concatenate([lo, hi, lo, hi], axis=1)
        h_ref[t] = spec[:Q]
        hn_ref[t] = spec[Q : Q + 8]
    out_ref[...] = jnp.full(out_ref.shape, -jnp.inf, F32)

    count = 4 * NB

    def chunk(k, carry):
        for b in range(NB):
            o = k * NB + b
            for i, (t_ref, n_ref) in enumerate(((t0_ref, n0_ref), (t1_ref, n1_ref))):
                for r in range(0, Q, 16):
                    rows = slice(r, r + 16)
                    tr = t_ref[o, rows, :S].astype(F32)
                    ti = t_ref[o, rows, S:].astype(F32)
                    for t in range(2):
                        at = (b * 4 + i * 2 + t) * Q + r
                        hr, hi = h_ref[t, rows, :S], h_ref[t, rows, S:]
                        pr = tr * hr + ti * hi
                        pi = tr * hi - ti * hr
                        if r == 0:
                            nr, ni = n_ref[o, :, :S], n_ref[o, :, S:]
                            mr, mi = hn_ref[t, :, :S], hn_ref[t, :, S:]
                            pr0 = pr[:8] - (nr * mi - ni * mr)
                            pi0 = pi[:8] + (nr * mr + ni * mi)
                            pr = jnp.concatenate([pr0, pr[8:]], axis=0)
                            pi = jnp.concatenate([pi0, pi[8:]], axis=0)
                        pr, pi = pr.astype(BF), pi.astype(BF)
                        p_ref[0, at : at + 16, :Q] = pr[:, :Q]
                        p_ref[0, at : at + 16, Q:] = pi[:, :Q]
                        p_ref[1, at : at + 16, :Q] = pr[:, Q:]
                        p_ref[1, at : at + 16, Q:] = pi[:, Q:]
        e_ref[...] = dot(p_ref[0], inv1_ref[0])
        o_ref[...] = dot(p_ref[1], inv1_ref[1])
        for j in range(count):
            for r in range(0, Q, 16):
                at = j * Q + r
                for lane in (0, Q):
                    even = e_ref[at : at + 16, lane : lane + Q]
                    odd = o_ref[at : at + 16, lane : lane + Q]
                    q_ref[j, lane + r : lane + r + 16, :Q] = (even + odd).astype(BF)
                    q_ref[j, lane + r : lane + r + 16, Q:] = (even - odd).astype(BF)
        for j in range(count):
            c_ref[j] = dot(inv2_ref[...], q_ref[j])
            power = jnp.zeros((8, Q), F32)
            for r in range(0, S, RC):
                part = c_ref[j, r : r + RC]
                part = part * part
                power += jnp.sum((part[:, :Q] + part[:, Q:]).reshape(RC // 8, 8, Q), axis=0)
            s_ref[j] = power
        total = jnp.sum(jnp.sum(s_ref[...], axis=1), axis=1, keepdims=True)
        scale = lax.rsqrt(total * (1.0 / (S * S)) + 1e-06)
        scales = [jnp.broadcast_to(scale[j : j + 1], (8, Q)) for j in range(count)]
        for t in range(2):
            for r in range(0, S, RC):
                spots = [(r + a, l * Q) for a in range(0, RC, 8) for l in range(2)]
                view = [
                    (row // 16, t, slice(row % 16, row % 16 + 8), slice(lane, lane + Q))
                    for row, lane in spots
                ]
                best = [out_ref[v] for v in view]
                for j in range(t, count, 2):
                    for i, (row, lane) in enumerate(spots):
                        corr = c_ref[j, row : row + 8, lane : lane + Q]
                        best[i] = jnp.maximum(best[i], corr * scales[j])
                for v, value in zip(view, best):
                    out_ref[v] = value
        return carry

    lax.fori_loop(0, OD // NB, chunk, 0)


def shards(tile_images, templates, filters, tile_bins):
    row, col, trow, tcol, inv1, inv2 = [jnp.asarray(a) for a in constants()]
    index = lax.axis_index(("yh", "x", "z", "yl", "c")).reshape(1)
    swap = [(0, 1), (1, 0)]
    ring = lambda s: [(i, (i + s) % 4) for i in range(4)]
    smem = pl.BlockSpec(memory_space=pltpu.SMEM)
    vmem = pl.BlockSpec(memory_space=pltpu.VMEM)
    hbm = pl.BlockSpec(memory_space=pltpu.HBM)
    tie = lax.optimization_barrier

    def spectra(t):
        return pl.pallas_call(
            template_kernel,
            out_shape=(
                jax.ShapeDtypeStruct((OD, Q, 2 * S), BF),
                jax.ShapeDtypeStruct((OD, 8, 2 * S), F32),
            ),
            in_specs=[vmem, vmem, vmem],
            out_specs=(vmem, vmem),
            scratch_shapes=[pltpu.VMEM((OD, 2 * Q, 2 * S), BF)],
            compiler_params=pltpu.CompilerParams(vmem_limit_bytes=16 * MIB),
            cost_estimate=pl.CostEstimate(
                flops=OD * 90_000_000, bytes_accessed=2_000_000, transcendentals=0
            ),
            name="templates",
        )(t, trow, tcol)

    like = lambda a: jax.ShapeDtypeStruct(a.shape, a.dtype)
    far = lambda a: pltpu.with_memory_space_constraint(a, pltpu.HBM)
    fil, img, own_templates, trow, tcol = pl.pallas_call(
        prep_kernel,
        out_shape=(
            jax.ShapeDtypeStruct((HR, Q), BF),
            jax.ShapeDtypeStruct((2, 2, 16, S), BF),
            like(templates),
            like(trow),
            like(tcol),
        ),
        in_specs=[smem] + [hbm] * 5,
        out_specs=(vmem,) * 5,
        scratch_shapes=[
            pltpu.VMEM((1, S, S), F32),
            pltpu.VMEM((4, 16, S), BF),
            pltpu.SemaphoreType.DMA((5,)),
        ],
        compiler_params=pltpu.CompilerParams(vmem_limit_bytes=8 * MIB),
        name="prep",
    )(index, far(filters), far(tile_images), far(templates), far(trow), far(tcol))
    near, across = [(0, 1), (1, 0), (2, 3), (3, 2)], [(0, 3), (3, 0), (1, 2), (2, 1)]
    fil_y = lax.ppermute(fil, ("yh", "yl"), across)
    img_z = lax.ppermute(img, "z", near)
    other_templates = lax.ppermute(own_templates, "c", swap)
    t0, n0 = spectra(own_templates)
    fil_y, t0, n0 = tie((fil_y, t0, n0))
    fil = jnp.stack([fil, fil_y])
    img = jnp.stack([img, img_z], axis=1)
    fil_x = lax.ppermute(fil, "x", near)
    img_z = lax.ppermute(img, "z", across)
    t1, n1 = spectra(other_templates)
    fil_x, t1, n1 = tie((fil_x, t1, n1))
    fil = jnp.stack([fil, fil_x])
    img = jnp.stack([img, img_z], axis=1)
    fil_x = lax.ppermute(fil, "x", across)
    img_y = lax.ppermute(img, "yl", swap)
    fil_a = jnp.stack([fil, fil_x])
    img_a = jnp.stack([img, img_y], axis=1)
    img_b = lax.ppermute(img_a[1], "c", swap)
    fil_b = lax.ppermute(fil_a, "c", swap)
    spec = pl.pallas_call(
        tile_kernel,
        out_shape=jax.ShapeDtypeStruct((2, HR, 2 * S), F32),
        in_specs=[smem] + [vmem] * 4,
        out_specs=vmem,
        scratch_shapes=[pltpu.VMEM((2, S, S), BF), pltpu.VMEM((2, 2 * S, 2 * S), BF)],
        compiler_params=pltpu.CompilerParams(vmem_limit_bytes=8 * MIB),
        cost_estimate=pl.CostEstimate(
            flops=800_000_000, bytes_accessed=1_000_000, transcendentals=0
        ),
        name="tiles",
    )(index, img_a[0], img_b, row, col)
    fil_b, spec = tie((fil_b, spec))

    count = 4 * NB
    part = pl.pallas_call(
        main_kernel,
        out_shape=jax.ShapeDtypeStruct((16, 2, 16, S), F32),
        in_specs=[smem, smem] + [vmem] * 9,
        out_specs=vmem,
        scratch_shapes=[
            pltpu.VMEM((2, Q, 2 * S), F32),
            pltpu.VMEM((2, 8, 2 * S), F32),
            pltpu.VMEM((2, count * Q, S), BF),
            pltpu.VMEM((count * Q, S), F32),
            pltpu.VMEM((count * Q, S), F32),
            pltpu.VMEM((count, S, S), BF),
            pltpu.VMEM((count, S, S), F32),
            pltpu.VMEM((count, 8, Q), F32),
        ],
        compiler_params=pltpu.CompilerParams(vmem_limit_bytes=24 * MIB),
        name="correlate",
    )(index, tile_bins, spec, fil_a, fil_b, t0, t1, n0, n1, inv1, inv2)

    got = lax.all_to_all(part.astype(jnp.float16), ("z", "yl", "c"), 0, 0)
    return jnp.max(got.astype(F32).reshape(8, 4, 16, S), axis=0)


def solution(mesh):
    fine = Mesh(mesh.devices.reshape(2, 4, 4, 2, 2), ("yh", "x", "z", "yl", "c"))
    tile, orient = ("yh", "x"), ("z", "yl", "c")
    placed = (P(tile, orient, None), P(orient, None, None), P(tile, None, None), P())
    return jax.shard_map(
        shards, mesh=fine, in_specs=placed, out_specs=P(tile, orient, None), check_vma=False
    )
```

```python
import jax
import jax.numpy as jnp
import ml_dtypes
import numpy as np
from jax import lax
from jax.experimental import pallas as pl
from jax.experimental.pallas import tpu as pltpu
from jax.sharding import Mesh
from jax.sharding import PartitionSpec as P

BF = jnp.bfloat16
F32 = jnp.float32
S = 256
Q = 128
HR = 144
OD = 12
NB = 3
RC = 32
MIB = 1024 * 1024


def tables():
    idx = np.arange(S)
    phase = 2.0 * np.pi * ((idx[:, None] * idx[None, :]) % S) / S
    cos = np.cos(phase).astype(ml_dtypes.bfloat16).astype(np.float32)
    sin = np.sin(phase).astype(ml_dtypes.bfloat16).astype(np.float32)
    return cos, sin


def constants():
    c, s = tables()
    cat = np.concatenate
    bf = lambda a: np.asarray(a, np.float32).astype(ml_dtypes.bfloat16)
    even, odd = np.arange(0, S, 2), np.arange(1, S, 2)
    order = cat([even, odd])
    row = bf(cat([c[:, order], -s[:, order]], 1))
    col = bf(cat([c, s], 1)[:HR])
    trow = bf(cat([c[:Q, order], -s[:Q, order]], 1))
    tcol = bf(cat([c[:, :Q], s[:, :Q]], 1)[:HR])
    turn = lambda k: cat([cat([c[k, :Q], s[k, :Q]], 1), cat([-s[k, :Q], c[k, :Q]], 1)], 0)
    inv1 = bf(np.stack([turn(even), turn(odd)]))
    wre = 2.0 * c[:, :Q]
    wre[:, 0] = c[:, 0]
    wim = -2.0 * s[:, :Q]
    wim[:, 0] = c[:, Q]
    inv2 = bf(cat([wre, wim], 1))
    return row, col, trow, tcol, inv1, inv2


def dot(a, b):
    return jnp.dot(a, b, preferred_element_type=F32)


def place(index):
    return index // 64, index // 16 % 4, index // 4 % 4, index // 2 % 2, index % 2


def fetch(pairs, sems):
    copies = [pltpu.make_async_copy(a, b, sems.at[i]) for i, (a, b) in enumerate(pairs)]
    for copy in copies:
        copy.start()
    return copies


def prep_kernel(
    index_ref, f_hbm, img_hbm, t_hbm, trow_hbm, tcol_hbm,
    fil_ref, split_ref, t_ref, trow_ref, tcol_ref,
    f_ref, img_ref, sems,
):
    core = index_ref[0] % 2
    copies = fetch(
        [
            (img_hbm, img_ref),
            (f_hbm, f_ref),
            (t_hbm, t_ref),
            (trow_hbm, trow_ref),
            (tcol_hbm, tcol_ref),
        ],
        sems,
    )
    a = lax.broadcasted_iota(jnp.int32, (S, S), 0)
    b = lax.broadcasted_iota(jnp.int32, (S, S), 1)
    ordered = jnp.where(b < Q, 2 * b, 2 * b - (S - 1))
    pick = lambda mask: jnp.where(mask, 1.0, 0.0).astype(BF)
    flip = pick((a + b) % S == 0)[:HR]
    same, turned = pick(a == ordered), pick((a + ordered) % S == 0)
    copies[0].wait()
    split_ref[0] = img_ref[pl.ds(2 * core, 2)]
    split_ref[1] = img_ref[pl.ds(2 - 2 * core, 2)]
    copies[1].wait()
    f = f_ref[0]
    hi = f.astype(BF)
    lo = (f - hi.astype(F32)).astype(BF)
    both = dot(flip, jnp.concatenate([hi, lo], axis=1)).astype(BF)
    terms = jnp.concatenate([hi[:HR], lo[:HR], both], axis=1)
    sums = dot(terms, jnp.concatenate([same, same, turned, turned], axis=0))
    sym = (0.5 * sums).astype(BF)
    fil_ref[...] = jnp.where(core == 0, sym[:, :Q], sym[:, Q:])
    for copy in copies[2:]:
        copy.wait()


def template_kernel(t_ref, trow_ref, tcol_ref, out_ref, nyq_ref, rhs_ref):
    count = t_ref.shape[0]
    rows = dot(t_ref[...].reshape(count * Q, Q), trow_ref[...]).astype(BF)
    for o in range(count):
        re = rows[o * Q : (o + 1) * Q, :S]
        im = rows[o * Q : (o + 1) * Q, S:]
        rhs_ref[o, :Q, :S] = re
        rhs_ref[o, :Q, S:] = im
        rhs_ref[o, Q:, :S] = im
        rhs_ref[o, Q:, S:] = -re
    first = lax.broadcasted_iota(jnp.int32, (8, 2 * S), 0) == 0
    for o in range(count):
        spec = dot(tcol_ref[...], rhs_ref[o])
        out_ref[o] = spec[:Q].astype(BF)
        nyq_ref[o] = jnp.where(first, spec[Q : Q + 8].astype(BF).astype(F32), 0.0)


def tile_kernel(index_ref, *refs):
    imgs, (row_ref, col_ref, spec_ref, x_ref, r_ref) = refs[:2], refs[2:]
    _, _, z, yl, core = place(index_ref[0])
    for t in range(2):
        for zs in range(4):
            for ys in range(2):
                for cs in range(2):
                    side = z if zs < 2 else 3 - z
                    if zs % 2:
                        side = side + 1 - side % 2 * 2
                    block = side * 4 + (yl + ys) % 2 * 2 + (core + cs) % 2
                    at = pl.multiple_of(block * 16, 16)
                    x_ref[t, pl.ds(at, 16), :] = imgs[cs][ys, zs // 2, zs % 2, t]
    for t in range(2):
        rows = dot(x_ref[t], row_ref[...]).astype(BF)
        re, im = rows[:, :S], rows[:, S:]
        r_ref[t, :S, :S] = re
        r_ref[t, :S, S:] = im
        r_ref[t, S:, :S] = im
        r_ref[t, S:, S:] = -re
    for t in range(2):
        spec_ref[t] = dot(col_ref[...], r_ref[t])


def main_kernel(
    index_ref, bins_ref, spec_ref, fa_ref, fb_ref,
    t0_ref, t1_ref, n0_ref, n1_ref, inv1_ref, inv2_ref,
    out_ref,
    h_ref, hn_ref, p_ref, e_ref, o_ref, q_ref, c_ref, s_ref,
):
    yh, x, _, _, core = place(index_ref[0])
    for t in range(2):
        name = bins_ref[(yh * 4 + x) * 4 + 2 * core + t]
        xs = (x // 2 + name % 4 // 2) % 2
        xn = (x + name + xs) % 2
        ys = (name // 4 + yh) % 2
        fa = fa_ref[xs, xn, ys].astype(F32)
        fb = fb_ref[xs, xn, ys].astype(F32)
        lo = jnp.where(core == 0, fa, fb)
        hi = jnp.where(core == 0, fb, fa)
        spec = spec_ref[t] * jnp.concatenate([lo, hi, lo, hi], axis=1)
        h_ref[t] = spec[:Q]
        hn_ref[t] = spec[Q : Q + 8]
    out_ref[...] = jnp.full(out_ref.shape, -jnp.inf, F32)

    count = 4 * NB

    def chunk(k, carry):
        for b in range(NB):
            o = k * NB + b
            for i, (t_ref, n_ref) in enumerate(((t0_ref, n0_ref), (t1_ref, n1_ref))):
                for r in range(0, Q, 16):
                    rows = slice(r, r + 16)
                    tr = t_ref[o, rows, :S].astype(F32)
                    ti = t_ref[o, rows, S:].astype(F32)
                    for t in range(2):
                        at = (b * 4 + i * 2 + t) * Q + r
                        hr, hi = h_ref[t, rows, :S], h_ref[t, rows, S:]
                        pr = tr * hr + ti * hi
                        pi = tr * hi - ti * hr
                        if r == 0:
                            nr, ni = n_ref[o, :, :S], n_ref[o, :, S:]
                            mr, mi = hn_ref[t, :, :S], hn_ref[t, :, S:]
                            pr0 = pr[:8] - (nr * mi - ni * mr)
                            pi0 = pi[:8] + (nr * mr + ni * mi)
                            pr = jnp.concatenate([pr0, pr[8:]], axis=0)
                            pi = jnp.concatenate([pi0, pi[8:]], axis=0)
                        pr, pi = pr.astype(BF), pi.astype(BF)
                        p_ref[0, at : at + 16, :Q] = pr[:, :Q]
                        p_ref[0, at : at + 16, Q:] = pi[:, :Q]
                        p_ref[1, at : at + 16, :Q] = pr[:, Q:]
                        p_ref[1, at : at + 16, Q:] = pi[:, Q:]
        e_ref[...] = dot(p_ref[0], inv1_ref[0])
        o_ref[...] = dot(p_ref[1], inv1_ref[1])
        for j in range(count):
            for r in range(0, Q, 16):
                at = j * Q + r
                for lane in (0, Q):
                    even = e_ref[at : at + 16, lane : lane + Q]
                    odd = o_ref[at : at + 16, lane : lane + Q]
                    q_ref[j, lane + r : lane + r + 16, :Q] = (even + odd).astype(BF)
                    q_ref[j, lane + r : lane + r + 16, Q:] = (even - odd).astype(BF)
        for j in range(count):
            c_ref[j] = dot(inv2_ref[...], q_ref[j])
            power = jnp.zeros((8, Q), F32)
            for r in range(0, S, RC):
                part = c_ref[j, r : r + RC]
                part = part * part
                power += jnp.sum((part[:, :Q] + part[:, Q:]).reshape(RC // 8, 8, Q), axis=0)
            s_ref[j] = power
        total = jnp.sum(jnp.sum(s_ref[...], axis=1), axis=1, keepdims=True)
        scale = lax.rsqrt(total * (1.0 / (S * S)) + 1e-06)
        scales = [jnp.broadcast_to(scale[j : j + 1], (8, Q)) for j in range(count)]
        for t in range(2):
            for r in range(0, S, RC):
                spots = [(r + a, l * Q) for a in range(0, RC, 8) for l in range(2)]
                view = [
                    (row // 16, t, slice(row % 16, row % 16 + 8), slice(lane, lane + Q))
                    for row, lane in spots
                ]
                best = [out_ref[v] for v in view]
                for j in range(t, count, 2):
                    for i, (row, lane) in enumerate(spots):
                        corr = c_ref[j, row : row + 8, lane : lane + Q]
                        best[i] = jnp.maximum(best[i], corr * scales[j])
                for v, value in zip(view, best):
                    out_ref[v] = value
        return carry

    lax.fori_loop(0, OD // NB, chunk, 0)


def shards(tile_images, templates, filters, tile_bins):
    row, col, trow, tcol, inv1, inv2 = [jnp.asarray(a) for a in constants()]
    index = lax.axis_index(("yh", "x", "z", "yl", "c")).reshape(1)
    swap = [(0, 1), (1, 0)]
    ring = lambda s: [(i, (i + s) % 4) for i in range(4)]
    smem = pl.BlockSpec(memory_space=pltpu.SMEM)
    vmem = pl.BlockSpec(memory_space=pltpu.VMEM)
    hbm = pl.BlockSpec(memory_space=pltpu.HBM)
    tie = lax.optimization_barrier

    def spectra(t):
        return pl.pallas_call(
            template_kernel,
            out_shape=(
                jax.ShapeDtypeStruct((OD, Q, 2 * S), BF),
                jax.ShapeDtypeStruct((OD, 8, 2 * S), F32),
            ),
            in_specs=[vmem, vmem, vmem],
            out_specs=(vmem, vmem),
            scratch_shapes=[pltpu.VMEM((OD, 2 * Q, 2 * S), BF)],
            compiler_params=pltpu.CompilerParams(vmem_limit_bytes=16 * MIB),
            cost_estimate=pl.CostEstimate(
                flops=OD * 90_000_000, bytes_accessed=2_000_000, transcendentals=0
            ),
            name="templates",
        )(t, trow, tcol)

    like = lambda a: jax.ShapeDtypeStruct(a.shape, a.dtype)
    far = lambda a: pltpu.with_memory_space_constraint(a, pltpu.HBM)
    fil, img, own_templates, trow, tcol = pl.pallas_call(
        prep_kernel,
        out_shape=(
            jax.ShapeDtypeStruct((HR, Q), BF),
            jax.ShapeDtypeStruct((2, 2, 16, S), BF),
            like(templates),
            like(trow),
            like(tcol),
        ),
        in_specs=[smem] + [hbm] * 5,
        out_specs=(vmem,) * 5,
        scratch_shapes=[
            pltpu.VMEM((1, S, S), F32),
            pltpu.VMEM((4, 16, S), BF),
            pltpu.SemaphoreType.DMA((5,)),
        ],
        compiler_params=pltpu.CompilerParams(vmem_limit_bytes=8 * MIB),
        name="prep",
    )(index, far(filters), far(tile_images), far(templates), far(trow), far(tcol))
    near, across = [(0, 1), (1, 0), (2, 3), (3, 2)], [(0, 3), (3, 0), (1, 2), (2, 1)]
    fil_y = lax.ppermute(fil, ("yh", "yl"), across)
    img_z = lax.ppermute(img, "z", near)
    other_templates = lax.ppermute(own_templates, "c", swap)
    t0, n0 = spectra(own_templates)
    fil_y, t0, n0 = tie((fil_y, t0, n0))
    fil = jnp.stack([fil, fil_y])
    img = jnp.stack([img, img_z], axis=1)
    fil_x = lax.ppermute(fil, "x", near)
    fil_w = lax.ppermute(fil, "x", across)
    img_z = lax.ppermute(img, "z", across)
    t1, n1 = spectra(other_templates)
    fil_x, t1, n1 = tie((fil_x, t1, n1))
    img = jnp.stack([img, img_z], axis=1)
    fil_v = lax.ppermute(fil_x, "x", across)
    img_y = lax.ppermute(img, "yl", swap)
    fil_a = jnp.stack([jnp.stack([fil, fil_x]), jnp.stack([fil_w, fil_v])])
    img_a = jnp.stack([img, img_y], axis=1)
    img_b = lax.ppermute(img_a[1], "c", swap)
    fil_b = lax.ppermute(fil_a, "c", swap)
    spec = pl.pallas_call(
        tile_kernel,
        out_shape=jax.ShapeDtypeStruct((2, HR, 2 * S), F32),
        in_specs=[smem] + [vmem] * 4,
        out_specs=vmem,
        scratch_shapes=[pltpu.VMEM((2, S, S), BF), pltpu.VMEM((2, 2 * S, 2 * S), BF)],
        compiler_params=pltpu.CompilerParams(vmem_limit_bytes=8 * MIB),
        cost_estimate=pl.CostEstimate(
            flops=800_000_000, bytes_accessed=1_000_000, transcendentals=0
        ),
        name="tiles",
    )(index, img_a[0], img_b, row, col)
    fil_b, spec = tie((fil_b, spec))

    count = 4 * NB
    part = pl.pallas_call(
        main_kernel,
        out_shape=jax.ShapeDtypeStruct((16, 2, 16, S), F32),
        in_specs=[smem, smem] + [vmem] * 9,
        out_specs=vmem,
        scratch_shapes=[
            pltpu.VMEM((2, Q, 2 * S), F32),
            pltpu.VMEM((2, 8, 2 * S), F32),
            pltpu.VMEM((2, count * Q, S), BF),
            pltpu.VMEM((count * Q, S), F32),
            pltpu.VMEM((count * Q, S), F32),
            pltpu.VMEM((count, S, S), BF),
            pltpu.VMEM((count, S, S), F32),
            pltpu.VMEM((count, 8, Q), F32),
        ],
        compiler_params=pltpu.CompilerParams(vmem_limit_bytes=24 * MIB),
        name="correlate",
    )(index, tile_bins, spec, fil_a, fil_b, t0, t1, n0, n1, inv1, inv2)

    got = lax.all_to_all(part.astype(jnp.float16), ("z", "yl", "c"), 0, 0)
    return jnp.max(got.astype(F32).reshape(8, 4, 16, S), axis=0)


def solution(mesh):
    fine = Mesh(mesh.devices.reshape(2, 4, 4, 2, 2), ("yh", "x", "z", "yl", "c"))
    tile, orient = ("yh", "x"), ("z", "yl", "c")
    placed = (P(tile, orient, None), P(orient, None, None), P(tile, None, None), P())
    return jax.shard_map(
        shards, mesh=fine, in_specs=placed, out_specs=P(tile, orient, None), check_vma=False
    )
```

```python
import jax
import jax.numpy as jnp
import ml_dtypes
import numpy as np
from jax import lax
from jax.experimental import pallas as pl
from jax.experimental.pallas import tpu as pltpu
from jax.sharding import Mesh
from jax.sharding import PartitionSpec as P

BF = jnp.bfloat16
F32 = jnp.float32
S = 256
Q = 128
HR = 144
OD = 12
NB = 3
RC = 32
MIB = 1024 * 1024


def tables():
    idx = np.arange(S)
    phase = 2.0 * np.pi * ((idx[:, None] * idx[None, :]) % S) / S
    cos = np.cos(phase).astype(ml_dtypes.bfloat16).astype(np.float32)
    sin = np.sin(phase).astype(ml_dtypes.bfloat16).astype(np.float32)
    return cos, sin


def constants():
    c, s = tables()
    cat = np.concatenate
    bf = lambda a: np.asarray(a, np.float32).astype(ml_dtypes.bfloat16)
    even, odd = np.arange(0, S, 2), np.arange(1, S, 2)
    order = cat([even, odd])
    row = bf(cat([c[:, order], -s[:, order]], 1))
    col = bf(cat([c, s], 1)[:HR])
    trow = bf(cat([c[:Q, order], -s[:Q, order]], 1))
    tcol = bf(cat([c[:, :Q], s[:, :Q]], 1)[:HR])
    turn = lambda k: cat([cat([c[k, :Q], s[k, :Q]], 1), cat([-s[k, :Q], c[k, :Q]], 1)], 0)
    inv1 = bf(np.stack([turn(even), turn(odd)]))
    wre = 2.0 * c[:, :Q]
    wre[:, 0] = c[:, 0]
    wim = -2.0 * s[:, :Q]
    wim[:, 0] = c[:, Q]
    inv2 = bf(cat([wre, wim], 1))
    return row, col, trow, tcol, inv1, inv2


def dot(a, b):
    return jnp.dot(a, b, preferred_element_type=F32)


def place(index):
    return index // 64, index // 16 % 4, index // 4 % 4, index // 2 % 2, index % 2


def fetch(pairs, sems):
    copies = [pltpu.make_async_copy(a, b, sems.at[i]) for i, (a, b) in enumerate(pairs)]
    for copy in copies:
        copy.start()
    return copies


def prep_kernel(
    index_ref, f_hbm, img_hbm, t_hbm, trow_hbm, tcol_hbm,
    fil_ref, split_ref, t_ref, trow_ref, tcol_ref,
    f_ref, img_ref, sems,
):
    core = index_ref[0] % 2
    copies = fetch(
        [
            (f_hbm, f_ref),
            (img_hbm, img_ref),
            (t_hbm, t_ref),
            (trow_hbm, trow_ref),
            (tcol_hbm, tcol_ref),
        ],
        sems,
    )
    a = lax.broadcasted_iota(jnp.int32, (S, S), 0)
    b = lax.broadcasted_iota(jnp.int32, (S, S), 1)
    ordered = jnp.where(b < Q, 2 * b, 2 * b - (S - 1))
    pick = lambda mask: jnp.where(mask, 1.0, 0.0).astype(BF)
    flip = pick((a + b) % S == 0)[:HR]
    same, turned = pick(a == ordered), pick((a + ordered) % S == 0)
    copies[0].wait()
    f = f_ref[0]
    hi = f.astype(BF)
    lo = (f - hi.astype(F32)).astype(BF)
    both = dot(flip, jnp.concatenate([hi, lo], axis=1)).astype(BF)
    terms = jnp.concatenate([hi[:HR], lo[:HR], both], axis=1)
    sums = dot(terms, jnp.concatenate([same, same, turned, turned], axis=0))
    sym = (0.5 * sums).astype(BF)
    fil_ref[...] = jnp.where(core == 0, sym[:, :Q], sym[:, Q:])
    copies[1].wait()
    split_ref[0] = img_ref[pl.ds(2 * core, 2)]
    split_ref[1] = img_ref[pl.ds(2 - 2 * core, 2)]
    for copy in copies[2:]:
        copy.wait()


def template_kernel(t_ref, trow_ref, tcol_ref, out_ref, nyq_ref, rhs_ref):
    count = t_ref.shape[0]
    rows = dot(t_ref[...].reshape(count * Q, Q), trow_ref[...]).astype(BF)
    for o in range(count):
        re = rows[o * Q : (o + 1) * Q, :S]
        im = rows[o * Q : (o + 1) * Q, S:]
        rhs_ref[o, :Q, :S] = re
        rhs_ref[o, :Q, S:] = im
        rhs_ref[o, Q:, :S] = im
        rhs_ref[o, Q:, S:] = -re
    first = lax.broadcasted_iota(jnp.int32, (8, 2 * S), 0) == 0
    for o in range(count):
        spec = dot(tcol_ref[...], rhs_ref[o])
        out_ref[o] = spec[:Q].astype(BF)
        nyq_ref[o] = jnp.where(first, spec[Q : Q + 8].astype(BF).astype(F32), 0.0)


def tile_kernel(index_ref, *refs):
    imgs, (row_ref, col_ref, spec_ref, x_ref, r_ref) = refs[:2], refs[2:]
    _, _, z, yl, core = place(index_ref[0])
    for t in range(2):
        for zs in range(4):
            for ys in range(2):
                for cs in range(2):
                    side = z if zs < 2 else 3 - z
                    if zs % 2:
                        side = side + 1 - side % 2 * 2
                    block = side * 4 + (yl + ys) % 2 * 2 + (core + cs) % 2
                    at = pl.multiple_of(block * 16, 16)
                    x_ref[t, pl.ds(at, 16), :] = imgs[cs][ys, zs // 2, zs % 2, t]
    for t in range(2):
        rows = dot(x_ref[t], row_ref[...]).astype(BF)
        re, im = rows[:, :S], rows[:, S:]
        r_ref[t, :S, :S] = re
        r_ref[t, :S, S:] = im
        r_ref[t, S:, :S] = im
        r_ref[t, S:, S:] = -re
    for t in range(2):
        spec_ref[t] = dot(col_ref[...], r_ref[t])


def main_kernel(
    index_ref, bins_ref, spec_ref, fa_ref, fb_ref,
    t0_ref, t1_ref, n0_ref, n1_ref, inv1_ref, inv2_ref,
    out_ref,
    h_ref, hn_ref, p_ref, e_ref, o_ref, q_ref, c_ref, s_ref,
):
    yh, x, _, _, core = place(index_ref[0])
    for t in range(2):
        name = bins_ref[(yh * 4 + x) * 4 + 2 * core + t]
        xs = (x // 2 + name % 4 // 2) % 2
        xn = (x + name + xs) % 2
        ys = (name // 4 + yh) % 2
        fa = fa_ref[xs, xn, ys].astype(F32)
        fb = fb_ref[xs, xn, ys].astype(F32)
        lo = jnp.where(core == 0, fa, fb)
        hi = jnp.where(core == 0, fb, fa)
        spec = spec_ref[t] * jnp.concatenate([lo, hi, lo, hi], axis=1)
        h_ref[t] = spec[:Q]
        hn_ref[t] = spec[Q : Q + 8]
    out_ref[...] = jnp.full(out_ref.shape, -jnp.inf, F32)

    count = 4 * NB

    def chunk(k, carry):
        for b in range(NB):
            o = k * NB + b
            for i, (t_ref, n_ref) in enumerate(((t0_ref, n0_ref), (t1_ref, n1_ref))):
                for r in range(0, Q, 16):
                    rows = slice(r, r + 16)
                    tr = t_ref[o, rows, :S].astype(F32)
                    ti = t_ref[o, rows, S:].astype(F32)
                    for t in range(2):
                        at = (b * 4 + i * 2 + t) * Q + r
                        hr, hi = h_ref[t, rows, :S], h_ref[t, rows, S:]
                        pr = tr * hr + ti * hi
                        pi = tr * hi - ti * hr
                        if r == 0:
                            nr, ni = n_ref[o, :, :S], n_ref[o, :, S:]
                            mr, mi = hn_ref[t, :, :S], hn_ref[t, :, S:]
                            pr0 = pr[:8] - (nr * mi - ni * mr)
                            pi0 = pi[:8] + (nr * mr + ni * mi)
                            pr = jnp.concatenate([pr0, pr[8:]], axis=0)
                            pi = jnp.concatenate([pi0, pi[8:]], axis=0)
                        pr, pi = pr.astype(BF), pi.astype(BF)
                        p_ref[0, at : at + 16, :Q] = pr[:, :Q]
                        p_ref[0, at : at + 16, Q:] = pi[:, :Q]
                        p_ref[1, at : at + 16, :Q] = pr[:, Q:]
                        p_ref[1, at : at + 16, Q:] = pi[:, Q:]
        e_ref[...] = dot(p_ref[0], inv1_ref[0])
        o_ref[...] = dot(p_ref[1], inv1_ref[1])
        for j in range(count):
            for r in range(0, Q, 16):
                at = j * Q + r
                for lane in (0, Q):
                    even = e_ref[at : at + 16, lane : lane + Q]
                    odd = o_ref[at : at + 16, lane : lane + Q]
                    q_ref[j, lane + r : lane + r + 16, :Q] = (even + odd).astype(BF)
                    q_ref[j, lane + r : lane + r + 16, Q:] = (even - odd).astype(BF)
        for j in range(count):
            c_ref[j] = dot(inv2_ref[...], q_ref[j])
            power = jnp.zeros((8, Q), F32)
            for r in range(0, S, RC):
                part = c_ref[j, r : r + RC]
                part = part * part
                power += jnp.sum((part[:, :Q] + part[:, Q:]).reshape(RC // 8, 8, Q), axis=0)
            s_ref[j] = power
        total = jnp.sum(jnp.sum(s_ref[...], axis=1), axis=1, keepdims=True)
        scale = lax.rsqrt(total * (1.0 / (S * S)) + 1e-06)
        scales = [jnp.broadcast_to(scale[j : j + 1], (8, Q)) for j in range(count)]
        for t in range(2):
            for r in range(0, S, RC):
                spots = [(r + a, l * Q) for a in range(0, RC, 8) for l in range(2)]
                view = [
                    (row // 16, t, slice(row % 16, row % 16 + 8), slice(lane, lane + Q))
                    for row, lane in spots
                ]
                best = [out_ref[v] for v in view]
                for j in range(t, count, 2):
                    for i, (row, lane) in enumerate(spots):
                        corr = c_ref[j, row : row + 8, lane : lane + Q]
                        best[i] = jnp.maximum(best[i], corr * scales[j])
                for v, value in zip(view, best):
                    out_ref[v] = value
        return carry

    lax.fori_loop(0, OD // NB, chunk, 0)


def shards(tile_images, templates, filters, tile_bins):
    row, col, trow, tcol, inv1, inv2 = [jnp.asarray(a) for a in constants()]
    index = lax.axis_index(("yh", "x", "z", "yl", "c")).reshape(1)
    swap = [(0, 1), (1, 0)]
    ring = lambda s: [(i, (i + s) % 4) for i in range(4)]
    smem = pl.BlockSpec(memory_space=pltpu.SMEM)
    vmem = pl.BlockSpec(memory_space=pltpu.VMEM)
    hbm = pl.BlockSpec(memory_space=pltpu.HBM)
    tie = lax.optimization_barrier

    def spectra(t):
        return pl.pallas_call(
            template_kernel,
            out_shape=(
                jax.ShapeDtypeStruct((OD, Q, 2 * S), BF),
                jax.ShapeDtypeStruct((OD, 8, 2 * S), F32),
            ),
            in_specs=[vmem, vmem, vmem],
            out_specs=(vmem, vmem),
            scratch_shapes=[pltpu.VMEM((OD, 2 * Q, 2 * S), BF)],
            compiler_params=pltpu.CompilerParams(vmem_limit_bytes=16 * MIB),
            cost_estimate=pl.CostEstimate(
                flops=OD * 90_000_000, bytes_accessed=2_000_000, transcendentals=0
            ),
            name="templates",
        )(t, trow, tcol)

    like = lambda a: jax.ShapeDtypeStruct(a.shape, a.dtype)
    far = lambda a: pltpu.with_memory_space_constraint(a, pltpu.HBM)
    fil, img, own_templates, trow, tcol = pl.pallas_call(
        prep_kernel,
        out_shape=(
            jax.ShapeDtypeStruct((HR, Q), BF),
            jax.ShapeDtypeStruct((2, 2, 16, S), BF),
            like(templates),
            like(trow),
            like(tcol),
        ),
        in_specs=[smem] + [hbm] * 5,
        out_specs=(vmem,) * 5,
        scratch_shapes=[
            pltpu.VMEM((1, S, S), F32),
            pltpu.VMEM((4, 16, S), BF),
            pltpu.SemaphoreType.DMA((5,)),
        ],
        compiler_params=pltpu.CompilerParams(vmem_limit_bytes=8 * MIB),
        name="prep",
    )(index, far(filters), far(tile_images), far(templates), far(trow), far(tcol))
    near, across = [(0, 1), (1, 0), (2, 3), (3, 2)], [(0, 3), (3, 0), (1, 2), (2, 1)]
    fil_y = lax.ppermute(fil, ("yh", "yl"), across)
    img_z = lax.ppermute(tile_images, "z", near).reshape(2, 2, 16, S)
    img_z = jnp.where(lax.axis_index("c") == 0, img_z, img_z[::-1])
    other_templates = lax.ppermute(own_templates, "c", swap)
    t0, n0 = spectra(own_templates)
    fil_y, t0, n0 = tie((fil_y, t0, n0))
    fil = jnp.stack([fil, fil_y])
    img = jnp.stack([img, img_z], axis=1)
    fil_x = lax.ppermute(fil, "x", near)
    fil_w = lax.ppermute(fil, "x", across)
    img_z = lax.ppermute(img, "z", across)
    t1, n1 = spectra(other_templates)
    fil_x, t1, n1 = tie((fil_x, t1, n1))
    img = jnp.stack([img, img_z], axis=1)
    fil_v = lax.ppermute(fil_x, "x", across)
    img_y = lax.ppermute(img, "yl", swap)
    fil_a = jnp.stack([jnp.stack([fil, fil_x]), jnp.stack([fil_w, fil_v])])
    img_a = jnp.stack([img, img_y], axis=1)
    img_b = lax.ppermute(img_a[1], "c", swap)
    fil_b = lax.ppermute(fil_a, "c", swap)
    spec = pl.pallas_call(
        tile_kernel,
        out_shape=jax.ShapeDtypeStruct((2, HR, 2 * S), F32),
        in_specs=[smem] + [vmem] * 4,
        out_specs=vmem,
        scratch_shapes=[pltpu.VMEM((2, S, S), BF), pltpu.VMEM((2, 2 * S, 2 * S), BF)],
        compiler_params=pltpu.CompilerParams(vmem_limit_bytes=8 * MIB),
        cost_estimate=pl.CostEstimate(
            flops=800_000_000, bytes_accessed=1_000_000, transcendentals=0
        ),
        name="tiles",
    )(index, img_a[0], img_b, row, col)
    fil_b, spec = tie((fil_b, spec))

    count = 4 * NB
    part = pl.pallas_call(
        main_kernel,
        out_shape=jax.ShapeDtypeStruct((16, 2, 16, S), F32),
        in_specs=[smem, smem] + [vmem] * 9,
        out_specs=vmem,
        scratch_shapes=[
            pltpu.VMEM((2, Q, 2 * S), F32),
            pltpu.VMEM((2, 8, 2 * S), F32),
            pltpu.VMEM((2, count * Q, S), BF),
            pltpu.VMEM((count * Q, S), F32),
            pltpu.VMEM((count * Q, S), F32),
            pltpu.VMEM((count, S, S), BF),
            pltpu.VMEM((count, S, S), F32),
            pltpu.VMEM((count, 8, Q), F32),
        ],
        compiler_params=pltpu.CompilerParams(vmem_limit_bytes=24 * MIB),
        name="correlate",
    )(index, tile_bins, spec, fil_a, fil_b, t0, t1, n0, n1, inv1, inv2)

    got = lax.all_to_all(part.astype(jnp.float16), ("z", "yl", "c"), 0, 0)
    return jnp.max(got.astype(F32).reshape(8, 4, 16, S), axis=0)


def solution(mesh):
    fine = Mesh(mesh.devices.reshape(2, 4, 4, 2, 2), ("yh", "x", "z", "yl", "c"))
    tile, orient = ("yh", "x"), ("z", "yl", "c")
    placed = (P(tile, orient, None), P(orient, None, None), P(tile, None, None), P())
    return jax.shard_map(
        shards, mesh=fine, in_specs=placed, out_specs=P(tile, orient, None), check_vma=False
    )
```
